768 devices in a mesh: ka: 192 (over x, z, y_lo), pt: 4 (over y_hi, core).
Axes of the slice: x: 4, y: 8 (y_hi: 2, y_lo: 4; y = y_hi * 4 + y_lo), z: 12, core: 2. Of those that a mesh axis runs over, the one named last changes fastest.
Arguments:
- orbitals: bfloat16 [192, 4096, 256], P('ka', 'pt'), may hold values from -6 to 6
- kernel: bfloat16 [192, 3, 256, 2, 4096], P('ka', None, None, None, 'pt'), may hold values from -0.00390625 to 0.00390625
- partners: int32 [192, 3], P('ka'), may hold values from 0 to 191, as said below
Outputs:
- exchanged: float32 [192, 256, 256], P('ka', 'pt')
The draws below stay inside these ranges and needn't reach their ends.
Inputs may be any that keep to these rules, and one draw needn't show every extreme that they name: partners[k, t] = (k - s_t) mod 192 for 3 distinct shifts s_t of 1 to 7, the same for every k; one of the shifts is 7.
All inputs are finite; a program needn't handle non-finite values.
Results may differ from the reference program's by a relative error of at most 0.0029.
Values may be sent and summed in bfloat16 or wider, within the bound.
No kernel may reach another device: no remote copies, remote signals or barrier semaphores. Data moves between devices by JAX's collectives and lax.ppermute only.
A program may use at most 32 MiB of HBM per device.

```python
import jax
import jax.numpy as jnp
from jax import lax

NP = 4096
NO = 128
MU_DEV = 64
TRANSFERS = 3
SPAN = 7
NK = 192
BLOCK = 1024
MU = 256


def draw_partners(key, part):
    key = jax.random.fold_in(key, 11)
    first_key, second_key = jax.random.split(key)
    smaller = (jax.random.permutation(first_key, SPAN - 1)[:TRANSFERS - 1] + 1).astype(jnp.int32)
    shifts = jnp.concatenate([smaller, jnp.array([SPAN], jnp.int32)])
    shifts = jax.random.permutation(second_key, shifts).astype(jnp.int32)
    kpoints = jnp.arange(NK, dtype=jnp.int32)[:, None]
    return ((kpoints - shifts[None, :]) % NK).astype(jnp.int32)


def block_scale(key, shape, cuts, low, largest):
    factor_of = 1.0
    for axis_at, parts in cuts:
        draws = jax.random.uniform(jax.random.fold_in(jax.random.fold_in(key, 6), axis_at), (parts,), jnp.float32, low / len(cuts), largest / len(cuts))
        factor_of = factor_of * jnp.repeat(jnp.exp(draws), shape[axis_at] // parts).reshape((-1,) + (1,) * (len(shape) - 1 - axis_at))
    return factor_of


def normal_values(own_key, extent, deviation, reach, cuts=(), held_as=jnp.bfloat16):
    result = jax.random.normal(own_key, extent, jnp.float32) * deviation
    if len(cuts) > 0:
        result = block_scale(own_key, extent, cuts, -0.22, 0.18) * result
    return jnp.clip(result, min=-reach, max=reach).astype(held_as)


def setup_inputs(seed: int = 0) -> dict:
    key_list = jax.random.split(jax.random.key(seed), 4)
    orbitals = normal_values(key_list[0], (NK, NP, 2 * NO), 1.0, 6.0, ((0, 192), (1, 4)))
    kernel = normal_values(key_list[1], (NK, TRANSFERS, MU, 2, NP), (4 * NO * NP) ** -0.5, 0.00390625, ((0, 192), (4, 4)))
    partners = draw_partners(jax.random.fold_in(key_list[3], 71), 0)
    return {"orbitals": orbitals, "kernel": kernel, "partners": partners}


def reference(orbitals, kernel, partners):
    positions = jnp.arange(MU, dtype=jnp.int32)
    window_index = ((positions // MU_DEV) * BLOCK + positions % MU_DEV).astype(jnp.int32)

    def exchange_for(kpoint):
        local_orbs = lax.dynamic_index_in_dim(orbitals, kpoint, 0, keepdims=False)
        turned = jnp.concatenate([local_orbs, jnp.concatenate([-local_orbs[:, NO:], local_orbs[:, :NO]], 1)], 0)
        kernel_here = lax.dynamic_index_in_dim(kernel, kpoint, 0, keepdims=False)
        summed = jnp.zeros((MU, 2 * NO), jnp.float32)
        for transfer in range(TRANSFERS):
            partner_index = partners[kpoint, transfer].astype(jnp.int32)
            partner_orbs = lax.dynamic_index_in_dim(orbitals, partner_index, 0, keepdims=False)
            window_part = jnp.take(partner_orbs, window_index, axis=0)
            swapped = jnp.concatenate([window_part[:, NO:], -window_part[:, :NO]], 1)
            density = jnp.dot(jnp.concatenate([window_part, swapped], 0), partner_orbs.T, preferred_element_type=jnp.float32)
            density_real = density[:MU]
            density_imag = density[MU:]
            kernel_real = kernel_here[transfer, :, 0, :].astype(jnp.float32)
            kernel_imag = kernel_here[transfer, :, 1, :].astype(jnp.float32)
            screened = jnp.concatenate([kernel_real * density_real - kernel_imag * density_imag, kernel_real * density_imag + kernel_imag * density_real], 1).astype(jnp.bfloat16)
            summed = summed + jnp.dot(screened, turned_whole(turned), preferred_element_type=jnp.float32)
        return summed

    return lax.map(exchange_for, jnp.arange(NK, dtype=jnp.int32))


def turned_whole(turned):
    upper = turned[:NP]
    lower = turned[NP:]
    return jnp.concatenate([upper, lower], 0)
```

```python
import functools

import jax
import jax.numpy as jnp
from jax import lax
from jax.experimental import pallas as pl
from jax.experimental.pallas import tpu as pltpu
from jax.sharding import PartitionSpec as P

MU_DEV = 64
TRANSFERS = 3
SPAN = 7
COLUMNS = 512

ROUTES = {
    (1, 2): {1: (0, 1), 2: (1, 1)},
    (2, 3): {3: (0, 3), 2: (3, -1)},
    (1, 5): {1: (0, 1), 5: (1, 4)},
    (2, 5): {1: (0, 1), 2: (1, 1), 5: (1, 4)},
    (4, 5): {4: (0, 4), 5: (4, 1)},
    (2, 6): {2: (0, 2), 6: (2, 4)},
    (3, 6): {3: (0, 3), 6: (3, 3)},
    (4, 6): {4: (0, 4), 6: (4, 2)},
    (5, 6): {5: (0, 5), 6: (5, 1)},
}


def passed_along(value, axis, steps):
    count = lax.axis_size(axis)
    pairs = [(source, (source + steps) % count) for source in range(count)]
    return lax.ppermute(value, axis, pairs)


def summed_over(partial, axis):
    count = lax.axis_size(axis)
    blocks = partial.reshape(count, partial.shape[0] // count, partial.shape[1])
    return jnp.sum(lax.all_to_all(blocks, axis, 0, 0), 0)


def arrivals(low, high, local_orbs):
    others = others_of(local_orbs[:MU_DEV], "pt")
    routes = ROUTES.get((low, high), {low: (0, low), high: (0, high)})
    held = {0: jnp.concatenate([local_orbs, others], 0)}
    for shift, (source, steps) in routes.items():
        held[shift] = passed_along(held[source], "ka", steps)
    return held[low], held[high], passed_along(others, "ka", SPAN)


def others_of(rows, axis):
    window = lax.all_gather(rows, axis, axis=0, tiled=True)
    start = (lax.axis_index(axis) + 1) * rows.shape[0]
    size = window.shape[0] - rows.shape[0]
    return lax.dynamic_slice_in_dim(jnp.concatenate([window, window], 0), start, size, 0)


def exchange_kernel(places_ref, far_ref, rest_ref, low_ref, high_ref, plane_ref, orbs_ref, out_ref, window_ref):
    transfer = pl.program_id(0)
    tile = pl.program_id(1)
    width = orbs_ref.shape[1]
    half_width = width // 2
    row_total = out_ref.shape[0]
    count = row_total // MU_DEV
    points = far_ref.shape[0]
    here = places_ref[TRANSFERS]
    columns = pl.ds(pl.multiple_of(tile * COLUMNS, COLUMNS), COLUMNS)

    def take_window(block_ref, others_ref, first_row):
        for steps in range(count):
            at = pl.multiple_of(lax.rem(here + steps, count) * MU_DEV, MU_DEV)
            start = first_row + (steps - 1) * MU_DEV
            rows = others_ref[start:start + MU_DEV, :] if steps else block_ref[0:MU_DEV, :]
            window_ref[pl.ds(at, MU_DEV), :] = rows
            window_ref[pl.ds(row_total + at, MU_DEV), 0:half_width] = rows[:, half_width:]
            window_ref[pl.ds(row_total + at, MU_DEV), half_width:width] = -rows[:, :half_width]

    def add_columns(block_ref):
        density = lax.dot_general(
            window_ref[...], block_ref[columns, :], (((1,), (1,)), ((), ())),
            preferred_element_type=jnp.float32,
        )
        density_real = density[:row_total]
        density_imag = density[row_total:]
        kernel_real = plane_ref[0, 0].astype(jnp.float32)
        kernel_imag = plane_ref[0, 1].astype(jnp.float32)
        screened_real = (kernel_real * density_real - kernel_imag * density_imag).astype(jnp.bfloat16)
        screened_imag = (kernel_real * density_imag + kernel_imag * density_real).astype(jnp.bfloat16)
        orbs = orbs_ref[columns, :]
        turned = jnp.concatenate([-orbs[:, half_width:], orbs[:, :half_width]], 1)
        out_ref[...] += jnp.dot(screened_real, orbs, preferred_element_type=jnp.float32) + jnp.dot(
            screened_imag, turned, preferred_element_type=jnp.float32
        )

    @pl.when((transfer == 0) & (tile == 0))
    def _():
        out_ref[...] = jnp.zeros_like(out_ref)

    arrived = ((far_ref, rest_ref, 0), (low_ref, low_ref, points), (high_ref, high_ref, points))
    for at, (block_ref, others_ref, first_row) in enumerate(arrived):

        @pl.when((transfer == at) & (tile == 0))
        def _(block_ref=block_ref, others_ref=others_ref, first_row=first_row):
            take_window(block_ref, others_ref, first_row)

        @pl.when(transfer == at)
        def _(block_ref=block_ref):
            add_columns(block_ref)


def exchanged_here(places, farthest, rest, low, high, planes, orbs):
    row_total, points = planes.shape[2:]
    width = orbs.shape[1]
    whole = pl.BlockSpec(memory_space=pltpu.VMEM)
    return pl.pallas_call(
        exchange_kernel,
        out_shape=jax.ShapeDtypeStruct((row_total, width), jnp.float32),
        grid_spec=pltpu.PrefetchScalarGridSpec(
            num_scalar_prefetch=1,
            grid=(TRANSFERS, points // COLUMNS),
            in_specs=[
                whole,
                whole,
                whole,
                whole,
                pl.BlockSpec((1, 2, row_total, COLUMNS), lambda t, c, places: (places[t], 0, 0, c)),
                whole,
            ],
            out_specs=pl.BlockSpec((row_total, width), lambda t, c, places: (0, 0)),
            scratch_shapes=[pltpu.VMEM((2 * row_total, width), jnp.bfloat16)],
        ),
        compiler_params=pltpu.CompilerParams(vmem_limit_bytes=24 * 2**20),
        cost_estimate=pl.CostEstimate(
            flops=2 * TRANSFERS * 4 * row_total * points * width,
            bytes_accessed=2 * planes.size + 2 * TRANSFERS * low.size,
            transcendentals=0,
        ),
    )(places, farthest, rest, low, high, planes, orbs)


def shards(orbitals, kernel, partners):
    local_orbs = orbitals[0]
    farthest = passed_along(local_orbs, "ka", SPAN)
    payload, planes = lax.optimization_barrier((local_orbs, kernel[0].transpose(0, 2, 1, 3)))
    here = lax.axis_index("ka")
    count = lax.axis_size("ka")
    shifts = [(here - partners[0, t] + count) % count for t in range(TRANSFERS)]
    smaller = [jnp.where(s == SPAN, 0, s) for s in shifts]
    high = jnp.maximum(jnp.maximum(smaller[0], smaller[1]), smaller[2])
    low = smaller[0] + smaller[1] + smaller[2] - high
    places = [
        jnp.where(shifts[1] == s, 1, 0) + jnp.where(shifts[2] == s, 2, 0) for s in (SPAN, low, high)
    ]
    places = jnp.stack(places + [lax.axis_index("pt")]).astype(jnp.int32)
    pairs = [(first, second) for second in range(2, SPAN) for first in range(1, second)]
    which = lax.shift_right_logical((high - 1) * (high - 2), 1) + low - 1
    branches = [functools.partial(arrivals, first, second) for first, second in pairs]
    from_low, from_high, rest = lax.switch(which, branches, payload)
    summed = exchanged_here(places, farthest, rest, from_low, from_high, planes, local_orbs)
    return summed_over(summed, "pt")[None]


def solution(mesh):
    in_specs = (P("ka", "pt", None), P("ka", None, None, None, "pt"), P("ka", None))
    out_specs = P("ka", "pt", None)
    return jax.shard_map(shards, mesh=mesh, in_specs=in_specs, out_specs=out_specs, check_vma=False)
```

```python
import functools

import jax
import jax.numpy as jnp
from jax import lax
from jax.experimental import pallas as pl
from jax.experimental.pallas import tpu as pltpu
from jax.sharding import PartitionSpec as P

MU_DEV = 64
TRANSFERS = 3
SPAN = 7
COLUMNS = 256

FIRST = 3
ROUTES = {
    (1, 2): ((2, 3), (1, 2)),
    (1, 3): ((1, 0),),
    (2, 3): ((2, 3),),
    (1, 4): ((2, 3), (4, 0), (1, 2)),
    (2, 4): ((2, 3), (4, 0)),
    (3, 4): ((4, 0),),
    (1, 5): ((1, 0), (5, 1)),
    (2, 5): ((2, 3), (5, 2)),
    (3, 5): ((2, 3), (5, 2)),
    (4, 5): ((4, 0), (5, 4)),
    (1, 6): ((6, 3), (1, 0)),
    (2, 6): ((6, 3), (2, 3)),
    (3, 6): ((6, 3),),
    (4, 6): ((6, 3), (4, 0)),
    (5, 6): ((6, 3), (5, 6)),
}


def passed_along(value, axis, steps):
    count = lax.axis_size(axis)
    pairs = [(source, (source + steps) % count) for source in range(count)]
    return lax.ppermute(value, axis, pairs)


def summed_over(partial, axis):
    count = lax.axis_size(axis)
    blocks = partial.reshape(count, partial.shape[0] // count, partial.shape[1])
    return jnp.sum(lax.all_to_all(blocks, axis, 0, 0).astype(jnp.float32), 0)


def arrivals(low, high, own, first):
    held = {0: own, FIRST: first}
    for shift, source in ROUTES[low, high]:
        held[shift] = passed_along(held[source], "ka", shift - source)
    return held[low], held[high]


def windows_of(blocks, axis):
    rows = jnp.concatenate([block[:MU_DEV] for block in blocks], 1)
    return lax.all_gather(rows, axis, axis=0, tiled=True)


def exchange_kernel(
    places_ref, far_ref, low_ref, high_ref, rows_ref, plane_ref, orbs_ref, out_ref, window_ref, sum_ref
):
    transfer = pl.program_id(0)
    points, width = orbs_ref.shape
    half_width = width // 2
    row_total = sum_ref.shape[0]

    def add_transfer(at, block_ref):
        real = rows_ref[:, at * width:at * width + half_width]
        imag = rows_ref[:, at * width + half_width:(at + 1) * width]
        window_ref[0:row_total, 0:half_width] = real
        window_ref[0:row_total, half_width:width] = imag
        window_ref[row_total:2 * row_total, 0:half_width] = imag
        window_ref[row_total:2 * row_total, half_width:width] = -real
        total = sum_ref[...]
        for tile in range(points // COLUMNS):
            columns = slice(tile * COLUMNS, (tile + 1) * COLUMNS)
            density = lax.dot_general(
                window_ref[...], block_ref[columns, :], (((1,), (1,)), ((), ())),
                preferred_element_type=jnp.float32,
            )
            density_real = density[:row_total]
            density_imag = density[row_total:]
            kernel_real = plane_ref[0, 0, :, columns].astype(jnp.float32)
            kernel_imag = plane_ref[0, 1, :, columns].astype(jnp.float32)
            screened_real = (kernel_real * density_real - kernel_imag * density_imag).astype(jnp.bfloat16)
            screened_imag = (kernel_real * density_imag + kernel_imag * density_real).astype(jnp.bfloat16)
            orbs = orbs_ref[columns, :]
            turned = jnp.concatenate([-orbs[:, half_width:], orbs[:, :half_width]], 1)
            total = total + jnp.dot(screened_real, orbs, preferred_element_type=jnp.float32)
            total = total + jnp.dot(screened_imag, turned, preferred_element_type=jnp.float32)
        sum_ref[...] = total

    @pl.when(transfer == 0)
    def _():
        sum_ref[...] = jnp.zeros_like(sum_ref)

    for at, block_ref in enumerate((far_ref, low_ref, high_ref)):

        @pl.when(transfer == at)
        def _(at=at, block_ref=block_ref):
            add_transfer(at, block_ref)

    @pl.when(transfer == TRANSFERS - 1)
    def _():
        out_ref[...] = sum_ref[...].astype(out_ref.dtype)


def exchanged_here(places, blocks, windows, planes, orbs):
    row_total, points = planes.shape[2:]
    width = orbs.shape[1]
    whole = pl.BlockSpec(memory_space=pltpu.VMEM)
    return pl.pallas_call(
        exchange_kernel,
        out_shape=jax.ShapeDtypeStruct((row_total, width), jnp.bfloat16),
        grid_spec=pltpu.PrefetchScalarGridSpec(
            num_scalar_prefetch=1,
            grid=(TRANSFERS,),
            in_specs=[whole] * (TRANSFERS + 1)
            + [pl.BlockSpec((1, 2, row_total, points), lambda t, places: (places[t], 0, 0, 0)), whole],
            out_specs=pl.BlockSpec((row_total, width), lambda t, places: (0, 0)),
            scratch_shapes=[
                pltpu.VMEM((2 * row_total, width), jnp.bfloat16),
                pltpu.VMEM((row_total, width), jnp.float32),
            ],
        ),
        compiler_params=pltpu.CompilerParams(vmem_limit_bytes=32 * 2**20),
        cost_estimate=pl.CostEstimate(
            flops=2 * TRANSFERS * 4 * row_total * points * width,
            bytes_accessed=2 * planes.size + 2 * TRANSFERS * orbs.size,
            transcendentals=0,
        ),
    )(places, *blocks, windows, planes, orbs)


def shards(orbitals, kernel, partners):
    local_orbs = orbitals[0]
    here = lax.axis_index("ka")
    count = lax.axis_size("ka")
    shifts = [(here - partners[0, t] + count) % count for t in range(TRANSFERS)]
    smaller = [jnp.where(s == SPAN, 0, s) for s in shifts]
    high = jnp.maximum(jnp.maximum(smaller[0], smaller[1]), smaller[2])
    low = smaller[0] + smaller[1] + smaller[2] - high
    places = [
        jnp.where(shifts[1] == s, 1, 0) + jnp.where(shifts[2] == s, 2, 0) for s in (SPAN, low, high)
    ]
    places = jnp.stack(places).astype(jnp.int32)
    which = lax.shift_right_logical((high - 1) * (high - 2), 1) + low - 1

    first = passed_along(local_orbs, "ka", FIRST)
    first, planes, places, which = lax.optimization_barrier(
        (first, kernel[0].transpose(0, 2, 1, 3), places, which)
    )
    farthest = passed_along(first, "ka", SPAN - FIRST)
    pairs = [(less, more) for more in range(2, SPAN) for less in range(1, more)]
    branches = [functools.partial(arrivals, less, more) for less, more in pairs]
    from_low, from_high = lax.switch(which, branches, local_orbs, first)
    blocks = (farthest, from_low, from_high)
    summed = exchanged_here(places, blocks, windows_of(blocks, "pt"), planes, local_orbs)
    return summed_over(summed, "pt")[None]


def solution(mesh):
    in_specs = (P("ka", "pt", None), P("ka", None, None, None, "pt"), P("ka", None))
    out_specs = P("ka", "pt", None)
    return jax.shard_map(shards, mesh=mesh, in_specs=in_specs, out_specs=out_specs, check_vma=False)
```

```python
import functools

import jax
import jax.numpy as jnp
from jax import lax
from jax.experimental import pallas as pl
from jax.experimental.pallas import tpu as pltpu
from jax.sharding import PartitionSpec as P

MU_DEV = 64
TRANSFERS = 3
SPAN = 7
COLUMNS = 256

FIRST = 3
ROUTES = {
    (1, 2): ((2, 3), (1, 2)),
    (1, 3): ((1, 0),),
    (2, 3): ((2, 3),),
    (1, 4): ((2, 3), (4, 0), (1, 2)),
    (2, 4): ((2, 3), (4, 0)),
    (3, 4): ((4, 0),),
    (1, 5): ((1, 0), (5, 1)),
    (2, 5): ((2, 3), (5, 2)),
    (3, 5): ((2, 3), (5, 2)),
    (4, 5): ((2, 3), (4, 0), (5, 2)),
    (1, 6): ((6, 3), (1, 0)),
    (2, 6): ((6, 3), (2, 3)),
    (3, 6): ((6, 3),),
    (4, 6): ((6, 3), (4, 0)),
    (5, 6): ((6, 3), (5, 6)),
}


def passed_along(value, axis, steps):
    count = lax.axis_size(axis)
    pairs = [(source, (source + steps) % count) for source in range(count)]
    return lax.ppermute(value, axis, pairs)


def summed_over(partial, axis):
    count = lax.axis_size(axis)
    blocks = partial.reshape(count, partial.shape[0] // count, partial.shape[1])
    return jnp.sum(lax.all_to_all(blocks, axis, 0, 0).astype(jnp.float32), 0)


def arrivals(low, high, own, first):
    held = {0: own, FIRST: first}
    for shift, source in ROUTES[low, high]:
        held[shift] = passed_along(held[source], "ka", shift - source)
    return held[low], held[high]


def rows_kernel(*refs):
    *block_refs, rows_ref, sems = refs
    width = rows_ref.shape[1] // len(block_refs)
    copies = [
        pltpu.make_async_copy(
            block_ref.at[0:MU_DEV, :], rows_ref.at[:, at * width:(at + 1) * width], sems.at[at]
        )
        for at, block_ref in enumerate(block_refs)
    ]
    for copy in copies:
        copy.start()
    for copy in copies:
        copy.wait()


def windows_of(blocks, axis):
    width = blocks[0].shape[1]
    rows = pl.pallas_call(
        rows_kernel,
        out_shape=jax.ShapeDtypeStruct((MU_DEV, len(blocks) * width), blocks[0].dtype),
        in_specs=[pl.BlockSpec(memory_space=pl.ANY)] * len(blocks),
        out_specs=pl.BlockSpec(memory_space=pltpu.VMEM),
        scratch_shapes=[pltpu.SemaphoreType.DMA((len(blocks),))],
    )(*blocks)
    return lax.all_gather(rows, axis, axis=0, tiled=True)


def exchange_kernel(
    places_ref, far_ref, low_ref, high_ref, rows_ref, plane_ref, orbs_ref, out_ref, window_ref, sum_ref
):
    transfer = pl.program_id(0)
    points, width = orbs_ref.shape
    half_width = width // 2
    row_total = sum_ref.shape[0]

    def add_transfer(at, block_ref):
        real = rows_ref[:, at * width:at * width + half_width]
        imag = rows_ref[:, at * width + half_width:(at + 1) * width]
        window_ref[0:row_total, 0:half_width] = real
        window_ref[0:row_total, half_width:width] = imag
        window_ref[row_total:2 * row_total, 0:half_width] = imag
        window_ref[row_total:2 * row_total, half_width:width] = -real
        total = sum_ref[...]
        for tile in range(points // COLUMNS):
            columns = slice(tile * COLUMNS, (tile + 1) * COLUMNS)
            density = lax.dot_general(
                window_ref[...], block_ref[columns, :], (((1,), (1,)), ((), ())),
                preferred_element_type=jnp.float32,
            )
            density_real = density[:row_total]
            density_imag = density[row_total:]
            kernel_real = plane_ref[0, 0, :, columns].astype(jnp.float32)
            kernel_imag = plane_ref[0, 1, :, columns].astype(jnp.float32)
            screened_real = (kernel_real * density_real - kernel_imag * density_imag).astype(jnp.bfloat16)
            screened_imag = (kernel_real * density_imag + kernel_imag * density_real).astype(jnp.bfloat16)
            orbs = orbs_ref[columns, :]
            turned = jnp.concatenate([-orbs[:, half_width:], orbs[:, :half_width]], 1)
            total = total + jnp.dot(screened_real, orbs, preferred_element_type=jnp.float32)
            total = total + jnp.dot(screened_imag, turned, preferred_element_type=jnp.float32)
        sum_ref[...] = total

    @pl.when(transfer == 0)
    def _():
        sum_ref[...] = jnp.zeros_like(sum_ref)

    for at, block_ref in enumerate((far_ref, low_ref, high_ref)):

        @pl.when(transfer == at)
        def _(at=at, block_ref=block_ref):
            add_transfer(at, block_ref)

    @pl.when(transfer == TRANSFERS - 1)
    def _():
        out_ref[...] = sum_ref[...].astype(out_ref.dtype)


def exchanged_here(places, blocks, windows, planes, orbs):
    row_total, points = planes.shape[2:]
    width = orbs.shape[1]
    whole = pl.BlockSpec(memory_space=pltpu.VMEM)
    return pl.pallas_call(
        exchange_kernel,
        out_shape=jax.ShapeDtypeStruct((row_total, width), jnp.bfloat16),
        grid_spec=pltpu.PrefetchScalarGridSpec(
            num_scalar_prefetch=1,
            grid=(TRANSFERS,),
            in_specs=[whole] * (TRANSFERS + 1)
            + [pl.BlockSpec((1, 2, row_total, points), lambda t, places: (places[t], 0, 0, 0)), whole],
            out_specs=pl.BlockSpec((row_total, width), lambda t, places: (0, 0)),
            scratch_shapes=[
                pltpu.VMEM((2 * row_total, width), jnp.bfloat16),
                pltpu.VMEM((row_total, width), jnp.float32),
            ],
        ),
        compiler_params=pltpu.CompilerParams(vmem_limit_bytes=32 * 2**20),
        cost_estimate=pl.CostEstimate(
            flops=2 * TRANSFERS * 4 * row_total * points * width,
            bytes_accessed=2 * planes.size + 2 * TRANSFERS * orbs.size,
            transcendentals=0,
        ),
    )(places, *blocks, windows, planes, orbs)


def shards(orbitals, kernel, partners):
    local_orbs = orbitals[0]
    here = lax.axis_index("ka")
    count = lax.axis_size("ka")
    shifts = [(here - partners[0, t] + count) % count for t in range(TRANSFERS)]
    smaller = [jnp.where(s == SPAN, 0, s) for s in shifts]
    high = jnp.maximum(jnp.maximum(smaller[0], smaller[1]), smaller[2])
    low = smaller[0] + smaller[1] + smaller[2] - high
    places = [
        jnp.where(shifts[1] == s, 1, 0) + jnp.where(shifts[2] == s, 2, 0) for s in (SPAN, low, high)
    ]
    places = jnp.stack(places).astype(jnp.int32)
    which = lax.shift_right_logical((high - 1) * (high - 2), 1) + low - 1

    first = passed_along(local_orbs, "ka", FIRST)
    first, planes, places, which = lax.optimization_barrier(
        (first, kernel[0].transpose(0, 2, 1, 3), places, which)
    )
    farthest = passed_along(first, "ka", SPAN - FIRST)
    pairs = [(less, more) for more in range(2, SPAN) for less in range(1, more)]
    branches = [functools.partial(arrivals, less, more) for less, more in pairs]
    from_low, from_high = lax.switch(which, branches, local_orbs, first)
    blocks = (farthest, from_low, from_high)
    summed = exchanged_here(places, blocks, windows_of(blocks, "pt"), planes, local_orbs)
    return summed_over(summed, "pt")[None]


def solution(mesh):
    in_specs = (P("ka", "pt", None), P("ka", None, None, None, "pt"), P("ka", None))
    out_specs = P("ka", "pt", None)
    return jax.shard_map(shards, mesh=mesh, in_specs=in_specs, out_specs=out_specs, check_vma=False)
```

```python
import functools

import jax
import jax.numpy as jnp
from jax import lax
from jax.experimental import pallas as pl
from jax.experimental.pallas import tpu as pltpu
from jax.sharding import PartitionSpec as P

MU_DEV = 64
TRANSFERS = 3
SPAN = 7
COLUMNS = 256

FIRST = 3
ROUTES = {
    (1, 2): ((1, 0), (2, 3)),
    (1, 3): ((1, 0),),
    (2, 3): ((2, 3),),
    (1, 4): ((2, 3), (4, 0), (1, 2)),
    (2, 4): ((2, 3), (4, 0)),
    (3, 4): ((4, 0),),
    (1, 5): ((1, 0), (5, 1)),
    (2, 5): ((2, 3), (5, 2)),
    (3, 5): ((2, 3), (5, 2)),
    (4, 5): ((2, 3), (4, 0), (5, 2)),
    (1, 6): ((6, 3), (1, 0)),
    (2, 6): ((6, 3), (2, 3)),
    (3, 6): ((6, 3),),
    (4, 6): ((6, 3), (4, 0)),
    (5, 6): ((6, 3), (5, 6)),
}


def passed_along(value, axis, steps):
    count = lax.axis_size(axis)
    pairs = [(source, (source + steps) % count) for source in range(count)]
    return lax.ppermute(value, axis, pairs)


def summed_over(partial, axis):
    count = lax.axis_size(axis)
    blocks = partial.reshape(count, partial.shape[0] // count, partial.shape[1])
    return jnp.sum(lax.all_to_all(blocks, axis, 0, 0).astype(jnp.float32), 0)


def arrivals(low, high, own, first):
    held = {0: own, FIRST: first}
    for shift, source in ROUTES[low, high]:
        held[shift] = passed_along(held[source], "ka", shift - source)
    return held[low], held[high]


def rows_kernel(*refs):
    *block_refs, rows_ref, sems = refs
    width = rows_ref.shape[1] // len(block_refs)
    copies = [
        pltpu.make_async_copy(
            block_ref.at[0:MU_DEV, :], rows_ref.at[:, at * width:(at + 1) * width], sems.at[at]
        )
        for at, block_ref in enumerate(block_refs)
    ]
    for copy in copies:
        copy.start()
    for copy in copies:
        copy.wait()


def windows_of(blocks, axis):
    width = blocks[0].shape[1]
    rows = pl.pallas_call(
        rows_kernel,
        out_shape=jax.ShapeDtypeStruct((MU_DEV, len(blocks) * width), blocks[0].dtype),
        in_specs=[pl.BlockSpec(memory_space=pl.ANY)] * len(blocks),
        out_specs=pl.BlockSpec(memory_space=pltpu.VMEM),
        scratch_shapes=[pltpu.SemaphoreType.DMA((len(blocks),))],
    )(*blocks)
    return lax.all_gather(rows, axis, axis=0, tiled=True)


def exchange_kernel(
    places_ref, far_ref, low_ref, high_ref, rows_ref, plane_ref, orbs_ref, out_ref, window_ref, sum_ref
):
    transfer = pl.program_id(0)
    points, width = orbs_ref.shape
    half_width = width // 2
    row_total = sum_ref.shape[0]

    def add_transfer(at, block_ref):
        real = rows_ref[:, at * width:at * width + half_width]
        imag = rows_ref[:, at * width + half_width:(at + 1) * width]
        window_ref[0:row_total, 0:half_width] = real
        window_ref[0:row_total, half_width:width] = imag
        window_ref[row_total:2 * row_total, 0:half_width] = imag
        window_ref[row_total:2 * row_total, half_width:width] = -real
        total = sum_ref[...]
        for tile in range(points // COLUMNS):
            columns = slice(tile * COLUMNS, (tile + 1) * COLUMNS)
            density = lax.dot_general(
                window_ref[...], block_ref[columns, :], (((1,), (1,)), ((), ())),
                preferred_element_type=jnp.float32,
            )
            density_real = density[:row_total]
            density_imag = density[row_total:]
            kernel_real = plane_ref[0, 0, :, columns].astype(jnp.float32)
            kernel_imag = plane_ref[0, 1, :, columns].astype(jnp.float32)
            screened_real = (kernel_real * density_real - kernel_imag * density_imag).astype(jnp.bfloat16)
            screened_imag = (kernel_real * density_imag + kernel_imag * density_real).astype(jnp.bfloat16)
            orbs = orbs_ref[columns, :]
            turned = jnp.concatenate([-orbs[:, half_width:], orbs[:, :half_width]], 1)
            total = total + jnp.dot(screened_real, orbs, preferred_element_type=jnp.float32)
            total = total + jnp.dot(screened_imag, turned, preferred_element_type=jnp.float32)
        sum_ref[...] = total

    @pl.when(transfer == 0)
    def _():
        sum_ref[...] = jnp.zeros_like(sum_ref)

    for at, block_ref in enumerate((far_ref, low_ref, high_ref)):

        @pl.when(transfer == at)
        def _(at=at, block_ref=block_ref):
            add_transfer(at, block_ref)

    @pl.when(transfer == TRANSFERS - 1)
    def _():
        out_ref[...] = sum_ref[...].astype(out_ref.dtype)


def exchanged_here(places, blocks, windows, planes, orbs):
    row_total, points = planes.shape[2:]
    width = orbs.shape[1]
    whole = pl.BlockSpec(memory_space=pltpu.VMEM)
    return pl.pallas_call(
        exchange_kernel,
        out_shape=jax.ShapeDtypeStruct((row_total, width), jnp.bfloat16),
        grid_spec=pltpu.PrefetchScalarGridSpec(
            num_scalar_prefetch=1,
            grid=(TRANSFERS,),
            in_specs=[whole] * (TRANSFERS + 1)
            + [pl.BlockSpec((1, 2, row_total, points), lambda t, places: (places[t], 0, 0, 0)), whole],
            out_specs=pl.BlockSpec((row_total, width), lambda t, places: (0, 0)),
            scratch_shapes=[
                pltpu.VMEM((2 * row_total, width), jnp.bfloat16),
                pltpu.VMEM((row_total, width), jnp.float32),
            ],
        ),
        compiler_params=pltpu.CompilerParams(vmem_limit_bytes=32 * 2**20),
        cost_estimate=pl.CostEstimate(
            flops=2 * TRANSFERS * 4 * row_total * points * width,
            bytes_accessed=2 * planes.size + 2 * TRANSFERS * orbs.size,
            transcendentals=0,
        ),
    )(places, *blocks, windows, planes, orbs)


def shards(orbitals, kernel, partners):
    local_orbs = orbitals[0]
    here = lax.axis_index("ka")
    count = lax.axis_size("ka")
    shifts = [(here - partners[0, t] + count) % count for t in range(TRANSFERS)]
    smaller = [jnp.where(s == SPAN, 0, s) for s in shifts]
    high = jnp.maximum(jnp.maximum(smaller[0], smaller[1]), smaller[2])
    low = smaller[0] + smaller[1] + smaller[2] - high
    places = [
        jnp.where(shifts[1] == s, 1, 0) + jnp.where(shifts[2] == s, 2, 0) for s in (SPAN, low, high)
    ]
    places = jnp.stack(places).astype(jnp.int32)
    which = lax.shift_right_logical((high - 1) * (high - 2), 1) + low - 1

    first = passed_along(local_orbs, "ka", FIRST)
    first, planes, places, which = lax.optimization_barrier(
        (first, kernel[0].transpose(0, 2, 1, 3), places, which)
    )
    farthest = passed_along(first, "ka", SPAN - FIRST)
    pairs = [(less, more) for more in range(2, SPAN) for less in range(1, more)]
    branches = [functools.partial(arrivals, less, more) for less, more in pairs]
    from_low, from_high = lax.switch(which, branches, local_orbs, first)
    blocks = (farthest, from_low, from_high)
    summed = exchanged_here(places, blocks, windows_of(blocks, "pt"), planes, local_orbs)
    return summed_over(summed, "pt")[None]


def solution(mesh):
    in_specs = (P("ka", "pt", None), P("ka", None, None, None, "pt"), P("ka", None))
    out_specs = P("ka", "pt", None)
    return jax.shard_map(shards, mesh=mesh, in_specs=in_specs, out_specs=out_specs, check_vma=False)
```
